32 devices in a mesh: depth: 4 (over y, x), front: 8 (over z, core).
Axes of the slice: x: 2, y: 2, z: 4, core: 2. Of those that a mesh axis runs over, the one named last changes fastest.
Arguments:
- inverse_factor: bfloat16 [4, 2, 8192, 8192], P('depth', None, 'front'), may hold values from -0.046875 to 0.046875
- coupling: float32 [4, 8192], P('depth', 'front'), may hold values from 0.3 to 1
- forcing: bfloat16 [4, 2, 48, 8192], P('depth', None, None, 'front'), may hold values from -6 to 6
- upper_trace: bfloat16 [2, 48, 8192], P(None, None, 'front'), may hold values from -6 to 6
Outputs:
- preconditioned: bfloat16 [4, 2, 48, 8192], P('depth', None, None, 'front')
The draws below stay inside these ranges and needn't reach their ends.
All inputs are finite; a program needn't handle non-finite values.
Results may differ from the reference program's by a relative error of at most 0.008.
Values may be sent and summed in bfloat16 or wider, within the bound.
No kernel may reach another device: no remote copies, remote signals or barrier semaphores. Data moves between devices by JAX's collectives and lax.ppermute only.
A program may use at most 64 MiB of HBM per device.

```python
import math
import jax
import jax.numpy as jnp

F = 8192
R = 48
LAYERS = 4


def block_scale(rng, extent, split, smallest, high):
    loudness = 1.0
    for axis_at, parts in split:
        heights = jax.random.uniform(jax.random.fold_in(jax.random.fold_in(rng, 6), axis_at), (parts,), jnp.float32, smallest / len(split), high / len(split))
        loudness = loudness * jnp.repeat(jnp.exp(heights), extent[axis_at] // parts).reshape((-1,) + (1,) * (len(extent) - 1 - axis_at))
    return loudness


def centred(stream_key, shape, deviation, most, cuts=(), dtype=jnp.bfloat16):
    factor_of = block_scale(stream_key, shape, cuts, -0.22, 0.18) if cuts else 1.0
    result = jax.random.normal(stream_key, shape, jnp.float32) * deviation * factor_of
    return jnp.minimum(jnp.maximum(result, -most), most).astype(dtype)


def setup_inputs(seed: int = 0) -> dict:
    arg_keys = jax.random.split(jax.random.key(seed), 5)
    return {
        "inverse_factor": centred(arg_keys[0], (LAYERS, 2, F, F), (2 * F) ** -0.5, 0.046875, ((0, 4), (2, 8))),
        "coupling": jnp.clip(jnp.exp(math.log(1.0) - 1.2039728 * jax.random.uniform(arg_keys[1], (LAYERS, F), jnp.float32) ** block_scale(arg_keys[1], (LAYERS, F), ((0, 4), (1, 8)), -0.2, 0.2)), 0.3, 1.0),
        "forcing": centred(arg_keys[2], (LAYERS, 2, R, F), 1.0, 6.0, ((0, 4), (3, 8))),
        "upper_trace": centred(arg_keys[3], (2, R, F), 1.0, 6.0, ((2, 8),)),
    }


def apply_inverse(matrix, vector):
    matrix_wide = matrix.astype(jnp.float32)
    vector_wide = vector.astype(jnp.float32)
    products = jnp.einsum("crk,dik->cdri", vector_wide, matrix_wide)
    real_part = products[0, 0] - products[1, 1]
    imag_part = products[1, 0] + products[0, 1]
    return jnp.stack([real_part, imag_part])


def reference(inverse_factor, coupling, forcing, upper_trace):
    layer_count = inverse_factor.shape[0]
    incoming = upper_trace
    downward = []
    for layer in range(layer_count):
        couple = coupling[layer].astype(jnp.float32)
        forced = (forcing[layer].astype(jnp.float32) - couple * incoming.astype(jnp.float32)).astype(jnp.bfloat16)
        solved = apply_inverse(inverse_factor[layer], forced).astype(jnp.bfloat16)
        downward.append(solved)
        incoming = solved
    upward = [None] * layer_count
    current = downward[layer_count - 1]
    upward[layer_count - 1] = current
    for layer in range(layer_count - 2, -1, -1):
        scaled = (coupling[layer + 1].astype(jnp.float32) * current.astype(jnp.float32)).astype(jnp.bfloat16)
        current = (downward[layer].astype(jnp.float32) - apply_inverse(inverse_factor[layer], scaled)).astype(jnp.bfloat16)
        upward[layer] = current
    return jnp.stack(upward)
```

```python
import functools

import jax
import jax.numpy as jnp
from jax import lax
from jax.experimental import pallas as pl
from jax.experimental.pallas import tpu as pltpu
from jax.sharding import PartitionSpec as P

VMEM = pl.BlockSpec(memory_space=pltpu.VMEM)
ANY = pl.BlockSpec(memory_space=pl.ANY)
KERNEL_VMEM = 12 << 20
AXES = ("depth", "front")


def passed_along(array, axis, by):
    peers = lax.axis_size(axis)
    pairs = [(i, i + by) for i in range(peers) if 0 <= i + by < peers]
    return lax.ppermute(array, axis, pairs)


def plain_body(inverse_factor, coupling, forcing, upper_trace):
    layer_index = lax.axis_index("depth")
    layer_count = lax.axis_size("depth")
    matrix = inverse_factor[0]
    couple = coupling[0]
    sources = forcing[0]

    def accumulate(segment):
        products = jnp.einsum("crk,dik->cdri", segment, matrix, preferred_element_type=jnp.float32)
        return jnp.stack([products[0, 0] - products[1, 1], products[1, 0] + products[0, 1]])

    downward = jnp.zeros_like(sources)
    outgoing = jnp.zeros_like(sources)
    for step in range(layer_count):
        incoming = upper_trace if step == 0 else passed_along(outgoing, "depth", 1)
        forced = (sources.astype(jnp.float32) - couple * incoming.astype(jnp.float32)).astype(jnp.bfloat16)
        outgoing = accumulate(lax.all_gather(forced, "front", axis=2, tiled=True)).astype(jnp.bfloat16)
        downward = jnp.where(layer_index == step, outgoing, downward)
    preconditioned = downward
    for step in range(layer_count - 2, -1, -1):
        scaled = (couple * preconditioned.astype(jnp.float32)).astype(jnp.bfloat16)
        incoming = passed_along(scaled, "depth", -1)
        correction = accumulate(lax.all_gather(incoming, "front", axis=2, tiled=True))
        updated = (downward.astype(jnp.float32) - correction).astype(jnp.bfloat16)
        preconditioned = jnp.where(layer_index == step, updated, preconditioned)
    return preconditioned[None]


def transpose_kernel(block, slots, g_ref, out_ref, held, sems):
    _, rows, depth = g_ref.shape
    per = depth // block
    count = 2 * per

    def copy(at, slot):
        part, col = at // per, lax.rem(at, per)
        window = pl.ds(pl.multiple_of(col * block, block), block)
        return pltpu.make_async_copy(g_ref.at[part, :, window], held.at[slot], sems.at[slot])

    for at in range(slots):
        copy(at, at).start()

    def turn(at, carry):
        slot = lax.rem(at, slots)
        copy(at, slot).wait()
        part, col = at // per, lax.rem(at, per)
        out_ref[part, pl.ds(pl.multiple_of(col * block, block), block), :] = held[slot].T

        @pl.when(at + slots < count)
        def _():
            copy(at + slots, slot).start()

        return carry

    lax.fori_loop(0, count, turn, 0)


def transposed(matrix):
    _, rows, depth = matrix.shape
    block, slots = 512, 4
    return pl.pallas_call(
        functools.partial(transpose_kernel, block, slots),
        out_shape=pltpu.VMEM((2, depth, rows), jnp.bfloat16),
        in_specs=[ANY],
        out_specs=VMEM,
        scratch_shapes=[pltpu.VMEM((slots, rows, block), jnp.bfloat16), pltpu.SemaphoreType.DMA((slots,))],
        compiler_params=pltpu.CompilerParams(vmem_limit_bytes=KERNEL_VMEM),
        cost_estimate=pl.CostEstimate(flops=0, bytes_accessed=matrix.size * 2, transcendentals=0),
        name="transpose_factor",
    )(matrix)


def parted(value, parts):
    out, at = [], 0
    for r in parts:
        out.append(jnp.concatenate([value[0, at : at + r], value[1, at : at + r]], axis=0).astype(jnp.bfloat16))
        at += r
    return out


def first_kernel(parts, forcing_ref, couple_ref, trace_ref, *outs):
    forcing = forcing_ref[...].astype(jnp.float32)
    forced = forcing - couple_ref[...][None] * trace_ref[...].astype(jnp.float32)
    for ref, piece in zip(outs, parted(forced, parts) + parted(forcing, parts), strict=True):
        ref[...] = piece


def first_vectors(forcing, couple, trace, parts):
    rows = forcing.shape[2]
    return pl.pallas_call(
        functools.partial(first_kernel, parts),
        out_shape=[jax.ShapeDtypeStruct((2 * r, rows), jnp.bfloat16) for r in parts * 2],
        in_specs=[VMEM] * 3,
        out_specs=[VMEM] * len(parts) * 2,
        compiler_params=pltpu.CompilerParams(vmem_limit_bytes=KERNEL_VMEM),
        name="first_forced",
    )(forcing, couple, trace)


def products(blocks, offsets, gt_ref, part, window):
    total = None
    for block, offset in zip(blocks, offsets, strict=True):
        depth = block.shape[1]
        columns = pl.ds(pl.multiple_of(offset * depth, depth), depth)
        term = jnp.dot(block[...], gt_ref[part, columns, window], preferred_element_type=jnp.float32)
        total = term if total is None else total + term
    return total


WIDE = 512


def partial_kernel(layer, shifts, resumed, gt_ref, *refs):
    blocks, refs = refs[: len(shifts)], refs[len(shifts) :]
    total_in = refs[0] if resumed else None
    total_out = refs[-1]
    rows = total_out.shape[2]

    @pl.when(lax.axis_index("depth") == layer)
    def _():
        me = lax.axis_index("front")
        offsets = [lax.bitwise_xor(me, jnp.int32(shift)) for shift in shifts]
        for part in range(2):
            for at in range(0, rows, WIDE):
                window = pl.ds(at, WIDE)
                value = products(blocks, offsets, gt_ref, part, window)
                total_out[part, :, window] = value if total_in is None else total_in[part, :, window] + value


def complex_of(blocks, offsets, gt_ref, total_ref, window):
    by_real = products(blocks, offsets, gt_ref, 0, window)
    by_imag = products(blocks, offsets, gt_ref, 1, window)
    if total_ref is not None:
        by_real += total_ref[0, :, window]
        by_imag += total_ref[1, :, window]
    r = by_real.shape[0] // 2
    return jnp.concatenate([by_real[:r] - by_imag[r:], by_real[r:] + by_imag[:r]], axis=0)


def last_kernel(layer, shifts, resumed, going_down, turning, gt_ref, *refs):
    blocks, refs = refs[: len(shifts)], refs[len(shifts) :]
    total_ref = refs[0] if resumed else None
    refs = refs[1:] if resumed else refs
    couple_ref, kept_ref, kept_out, sent_out = refs[0], refs[-3], refs[-2], refs[-1]
    other_ref = refs[1] if going_down else None
    rows = kept_out.shape[1]

    @pl.when(lax.axis_index("depth") == layer)
    def _():
        me = lax.axis_index("front")
        offsets = [lax.bitwise_xor(me, jnp.int32(shift)) for shift in shifts]
        for at in range(0, rows, WIDE):
            window = pl.ds(at, WIDE)
            value = complex_of(blocks, offsets, gt_ref, total_ref, window)
            couple = couple_ref[:, window]
            if going_down:
                kept = value.astype(jnp.bfloat16)
                wide = couple * kept.astype(jnp.float32)
                sent = wide if turning else other_ref[:, window].astype(jnp.float32) - wide
            else:
                kept = (kept_ref[:, window].astype(jnp.float32) - value).astype(jnp.bfloat16)
                sent = couple * kept.astype(jnp.float32)
            kept_out[:, window] = kept
            sent_out[:, window] = sent.astype(jnp.bfloat16)


def cost(blocks, gt):
    depth = sum(block.shape[1] for block in blocks)
    rows = gt.shape[2]
    return pl.CostEstimate(
        flops=4 * blocks[0].shape[0] * depth * rows, bytes_accessed=4 * depth * rows, transcendentals=0
    )


def partial_apply(layer, gt, blocks, shifts, total):
    resumed = total is not None
    shape = (2, blocks[0].shape[0], gt.shape[2])
    operands = [pltpu.with_memory_space_constraint(gt, pltpu.VMEM), *blocks]
    aliases = {}
    if resumed:
        aliases = {len(operands): 0}
        operands.append(pltpu.with_memory_space_constraint(total, pltpu.VMEM))
    return pl.pallas_call(
        functools.partial(partial_kernel, layer, shifts, resumed),
        out_shape=pltpu.VMEM(shape, jnp.float32),
        in_specs=[VMEM] * len(operands),
        out_specs=VMEM,
        input_output_aliases=aliases,
        compiler_params=pltpu.CompilerParams(vmem_limit_bytes=KERNEL_VMEM),
        cost_estimate=cost(blocks, gt),
        name="partial_apply",
    )(*operands)


def last_apply(layer, gt, blocks, shifts, total, couple, other, kept, going_down, turning):
    resumed = total is not None
    operands = [pltpu.with_memory_space_constraint(gt, pltpu.VMEM), *blocks]
    if resumed:
        operands.append(pltpu.with_memory_space_constraint(total, pltpu.VMEM))
    operands += [couple, other, kept] if going_down else [couple, kept]
    shape = jax.ShapeDtypeStruct(kept.shape, jnp.bfloat16)
    return pl.pallas_call(
        functools.partial(last_kernel, layer, shifts, resumed, going_down, turning),
        out_shape=[shape, shape],
        in_specs=[VMEM] * len(operands),
        out_specs=[VMEM] * 2,
        input_output_aliases={len(operands) - 1: 0},
        compiler_params=pltpu.CompilerParams(vmem_limit_bytes=KERNEL_VMEM),
        cost_estimate=cost(blocks, gt),
        name="last_apply",
    )(*operands)


def join_kernel(parts, *refs):
    ins, out_ref = refs[:-1], refs[-1]
    values = [ref[...].astype(jnp.float32) for ref in ins]
    for c in range(2):
        rows = [value[c * r : (c + 1) * r] for value, r in zip(values, parts, strict=True)]
        out_ref[c] = jnp.concatenate(rows, axis=0).astype(jnp.bfloat16)


def joined(pieces, parts):
    return pl.pallas_call(
        functools.partial(join_kernel, parts),
        out_shape=jax.ShapeDtypeStruct((2, sum(parts), pieces[0].shape[1]), jnp.bfloat16),
        in_specs=[VMEM] * len(parts),
        out_specs=VMEM,
        compiler_params=pltpu.CompilerParams(vmem_limit_bytes=KERNEL_VMEM),
        name="join_parts",
    )(*pieces)


def moved(array, layers, peers, rule):
    pairs = []
    for layer in range(layers):
        for place in range(peers):
            target = rule(layer, place)
            if target is not None:
                pairs.append((layer * peers + place, target[0] * peers + target[1]))
    return lax.ppermute(array, AXES, pairs)


def resident_body(layers, peers, parts, inverse_factor, coupling, forcing, upper_trace):
    chips = peers // 2

    def to_next(block, source, target, shift):
        return moved(
            block, layers, peers, lambda layer, place: (target, place ^ shift) if layer == source else None
        )

    def swap(block):
        return moved(block, layers, peers, lambda layer, place: (layer, place ^ 1))

    def up(array):
        return moved(array, layers, peers, lambda layer, place: (layer - 1, place) if layer else None)

    pieces = first_vectors(forcing[0], coupling, upper_trace, parts)
    first, own = pieces[: len(parts)], pieces[len(parts) :]
    sources_below, couple_below = [up(piece) for piece in own], up(coupling)

    def spread(vector, source, target):
        order = list(range(chips - 1, -1, -1))
        direct = [
            vector if source == target and not chip else to_next(vector, source, target, 2 * chip) for chip in order
        ]
        if source == target:
            order, direct = order[-1:] + order[:-1], direct[-1:] + direct[:-1]
        across = [swap(block) for block in direct]
        groups = [([direct[0]], [2 * order[0]])]
        for i in range(1, chips):
            groups.append(([across[i - 1], direct[i]], [2 * order[i - 1] + 1, 2 * order[i]]))
        groups.append(([across[-1]], [2 * order[-1] + 1]))
        return groups

    arrived = [spread(vector, 0, 0) for vector in first]
    gt = transposed(inverse_factor[0])

    def apply(layer, groups, couple, other, kept, going_down, turning):
        total = None
        for blocks, shifts in groups[:-1]:
            total = partial_apply(layer, gt, blocks, shifts, total)
        blocks, shifts = groups[-1]
        return last_apply(layer, gt, blocks, shifts, total, couple, other, kept, going_down, turning)

    solved = list(first)
    for layer in range(layers):
        turning = layer == layers - 1
        couple = coupling if turning else couple_below
        for i in range(len(parts)):
            solved[i], sent = apply(layer, arrived[i], couple, sources_below[i], solved[i], True, turning)
            if not turning or layers > 1:
                arrived[i] = spread(sent, layer, layer - 1 if turning else layer + 1)
    result = list(solved)
    for layer in range(layers - 2, -1, -1):
        for i in range(len(parts)):
            result[i], sent = apply(layer, arrived[i], coupling, None, result[i], False, False)
            if layer:
                arrived[i] = spread(sent, layer, layer - 1)
    return joined(result, parts)[None]


def cut(count):
    half = count // 2
    return (half, count - half) if count % 16 == 0 and count > 16 else (count,)


def solution(mesh):
    layers, peers = mesh.shape["depth"], mesh.shape["front"]
    placed = (
        P("depth", None, "front", None),
        P("depth", "front"),
        P("depth", None, None, "front"),
        P(None, None, "front"),
    )

    def body(inverse_factor, coupling, forcing, upper_trace):
        rows = inverse_factor.shape[2]
        fits = inverse_factor.size * 2 <= 40 << 20 and rows % WIDE == 0
        if fits and peers in (2, 4, 8):
            return resident_body(layers, peers, cut(forcing.shape[2]), inverse_factor, coupling, forcing, upper_trace)
        return plain_body(inverse_factor, coupling, forcing, upper_trace)

    return jax.shard_map(
        body, mesh=mesh, in_specs=placed, out_specs=P("depth", None, None, "front"), check_vma=False
    )
```

```python
import functools

import jax
import jax.numpy as jnp
from jax import lax
from jax.experimental import pallas as pl
from jax.experimental.pallas import tpu as pltpu
from jax.sharding import PartitionSpec as P

VMEM = pl.BlockSpec(memory_space=pltpu.VMEM)
ANY = pl.BlockSpec(memory_space=pl.ANY)
KERNEL_VMEM = 8 << 20
PRIORITY = 64
AXES = ("depth", "front")


def passed_along(array, axis, by):
    peers = lax.axis_size(axis)
    pairs = [(i, i + by) for i in range(peers) if 0 <= i + by < peers]
    return lax.ppermute(array, axis, pairs)


def plain_body(inverse_factor, coupling, forcing, upper_trace):
    layer_index = lax.axis_index("depth")
    layer_count = lax.axis_size("depth")
    matrix = inverse_factor[0]
    couple = coupling[0]
    sources = forcing[0]

    def accumulate(segment):
        products = jnp.einsum("crk,dik->cdri", segment, matrix, preferred_element_type=jnp.float32)
        return jnp.stack([products[0, 0] - products[1, 1], products[1, 0] + products[0, 1]])

    downward = jnp.zeros_like(sources)
    outgoing = jnp.zeros_like(sources)
    for step in range(layer_count):
        incoming = upper_trace if step == 0 else passed_along(outgoing, "depth", 1)
        forced = (sources.astype(jnp.float32) - couple * incoming.astype(jnp.float32)).astype(jnp.bfloat16)
        outgoing = accumulate(lax.all_gather(forced, "front", axis=2, tiled=True)).astype(jnp.bfloat16)
        downward = jnp.where(layer_index == step, outgoing, downward)
    preconditioned = downward
    for step in range(layer_count - 2, -1, -1):
        scaled = (couple * preconditioned.astype(jnp.float32)).astype(jnp.bfloat16)
        incoming = passed_along(scaled, "depth", -1)
        correction = accumulate(lax.all_gather(incoming, "front", axis=2, tiled=True))
        updated = (downward.astype(jnp.float32) - correction).astype(jnp.bfloat16)
        preconditioned = jnp.where(layer_index == step, updated, preconditioned)
    return preconditioned[None]


def transpose_kernel(block, slots, g_ref, out_ref, held, sems):
    _, rows, depth = g_ref.shape
    per = depth // block
    count = 2 * per

    def copy(at, slot):
        part, col = at // per, lax.rem(at, per)
        window = pl.ds(pl.multiple_of(col * block, block), block)
        return pltpu.make_async_copy(g_ref.at[part, :, window], held.at[slot], sems.at[slot])

    for at in range(slots):
        copy(at, at).start()

    def turn(at, carry):
        slot = lax.rem(at, slots)
        copy(at, slot).wait()
        part, col = at // per, lax.rem(at, per)
        out_ref[part, pl.ds(pl.multiple_of(col * block, block), block), :] = held[slot].T

        @pl.when(at + slots < count)
        def _():
            copy(at + slots, slot).start()

        return carry

    lax.fori_loop(0, count, turn, 0)


def transposed(matrix):
    _, rows, depth = matrix.shape
    block, slots = 512, 4
    return pl.pallas_call(
        functools.partial(transpose_kernel, block, slots),
        out_shape=pltpu.VMEM((2, depth, rows), jnp.bfloat16),
        in_specs=[ANY],
        out_specs=VMEM,
        scratch_shapes=[pltpu.VMEM((slots, rows, block), jnp.bfloat16), pltpu.SemaphoreType.DMA((slots,))],
        compiler_params=pltpu.CompilerParams(vmem_limit_bytes=KERNEL_VMEM),
        cost_estimate=pl.CostEstimate(flops=PRIORITY * 100 * matrix.size, bytes_accessed=matrix.size * 2, transcendentals=0),
        name="transpose_factor",
    )(matrix)


def first_kernel(forcing_ref, couple_ref, trace_ref, forced_out, pack_out):
    r = forcing_ref.shape[1]
    couple = couple_ref[...]
    for c in range(2):
        rows = pl.ds(c * r, r)
        forcing = forcing_ref[c].astype(jnp.float32)
        forced_out[rows, :] = (forcing - couple * trace_ref[c].astype(jnp.float32)).astype(jnp.bfloat16)
        pack_out[rows, :] = forcing
    pack_out[2 * r :, :] = jnp.broadcast_to(couple, (8, couple.shape[1]))


def first_vectors(forcing, couple, trace):
    _, r, rows = forcing.shape
    return pl.pallas_call(
        first_kernel,
        out_shape=[
            jax.ShapeDtypeStruct((2 * r, rows), jnp.bfloat16),
            jax.ShapeDtypeStruct((2 * r + 8, rows), jnp.float32),
        ],
        in_specs=[VMEM] * 3,
        out_specs=[VMEM] * 2,
        compiler_params=pltpu.CompilerParams(vmem_limit_bytes=KERNEL_VMEM),
        name="first_forced",
    )(forcing, couple, trace)


def products(blocks, offsets, gt_ref, part, window):
    total = None
    for block, offset in zip(blocks, offsets, strict=True):
        depth = block.shape[1]
        columns = pl.ds(pl.multiple_of(offset * depth, depth), depth)
        term = jnp.dot(block[...], gt_ref[part, columns, window], preferred_element_type=jnp.float32)
        total = term if total is None else total + term
    return total


WIDE = 512


def partial_kernel(layer, shifts, resumed, gt_ref, *refs):
    blocks, refs = refs[: len(shifts)], refs[len(shifts) :]
    total_in = refs[0] if resumed else None
    total_out = refs[-1]
    rows = total_out.shape[2]

    @pl.when(lax.axis_index("depth") == layer)
    def _():
        me = lax.axis_index("front")
        offsets = [lax.bitwise_xor(me, jnp.int32(shift)) for shift in shifts]
        for part in range(2):
            for at in range(0, rows, WIDE):
                window = pl.ds(at, WIDE)
                value = products(blocks, offsets, gt_ref, part, window)
                total_out[part, :, window] = value if total_in is None else total_in[part, :, window] + value


def complex_of(blocks, offsets, gt_ref, total_ref, window):
    by_real = products(blocks, offsets, gt_ref, 0, window)
    by_imag = products(blocks, offsets, gt_ref, 1, window)
    if total_ref is not None:
        by_real += total_ref[0, :, window]
        by_imag += total_ref[1, :, window]
    r = by_real.shape[0] // 2
    return jnp.concatenate([by_real[:r] - by_imag[r:], by_real[r:] + by_imag[:r]], axis=0)


def last_kernel(layer, shifts, resumed, going_down, turning, gt_ref, *refs):
    blocks, refs = refs[: len(shifts)], refs[len(shifts) :]
    total_ref = refs[0] if resumed else None
    refs = refs[1:] if resumed else refs
    couple_ref, kept_ref, kept_out, sent_out = refs
    rows = kept_out.shape[1]
    r = kept_out.shape[0]
    below = going_down and not turning

    @pl.when(lax.axis_index("depth") == layer)
    def _():
        me = lax.axis_index("front")
        offsets = [lax.bitwise_xor(me, jnp.int32(shift)) for shift in shifts]
        for at in range(0, rows, WIDE):
            window = pl.ds(at, WIDE)
            value = complex_of(blocks, offsets, gt_ref, total_ref, window)
            couple = couple_ref[r : r + 1, window] if below else couple_ref[:, window]
            if going_down:
                kept = value.astype(jnp.bfloat16)
                wide = couple * kept.astype(jnp.float32)
                sent = wide if turning else couple_ref[:r, window] - wide
            else:
                kept = (kept_ref[:, window].astype(jnp.float32) - value).astype(jnp.bfloat16)
                sent = couple * kept.astype(jnp.float32)
            kept_out[:, window] = kept
            sent_out[:, window] = sent.astype(jnp.bfloat16)


def near(array):
    return pltpu.with_memory_space_constraint(array, pltpu.VMEM)


def cost(blocks, gt):
    depth = sum(block.shape[1] for block in blocks)
    rows = gt.shape[2]
    return pl.CostEstimate(
        flops=PRIORITY * 4 * blocks[0].shape[0] * depth * rows, bytes_accessed=4 * depth * rows, transcendentals=0
    )


def partial_apply(layer, gt, blocks, shifts, total):
    resumed = total is not None
    shape = (2, blocks[0].shape[0], gt.shape[2])
    operands = [gt, *blocks]
    aliases = {}
    if resumed:
        aliases = {len(operands): 0}
        operands.append(total)
    operands = [near(array) for array in operands]
    return pl.pallas_call(
        functools.partial(partial_kernel, layer, shifts, resumed),
        out_shape=pltpu.VMEM(shape, jnp.float32),
        in_specs=[VMEM] * len(operands),
        out_specs=VMEM,
        input_output_aliases=aliases,
        compiler_params=pltpu.CompilerParams(vmem_limit_bytes=KERNEL_VMEM),
        cost_estimate=cost(blocks, gt),
        name="partial_apply",
    )(*operands)


def last_apply(layer, gt, blocks, shifts, total, couple, kept, going_down, turning):
    resumed = total is not None
    operands = [gt, *blocks, *([total] if resumed else []), couple, kept]
    operands = [near(array) for array in operands]
    shape = jax.ShapeDtypeStruct(kept.shape, jnp.bfloat16)
    return pl.pallas_call(
        functools.partial(last_kernel, layer, shifts, resumed, going_down, turning),
        out_shape=[shape, shape],
        in_specs=[VMEM] * len(operands),
        out_specs=[VMEM] * 2,
        input_output_aliases={len(operands) - 1: 0},
        compiler_params=pltpu.CompilerParams(vmem_limit_bytes=KERNEL_VMEM),
        cost_estimate=cost(blocks, gt),
        name="last_apply",
    )(*operands)


def nothing_kernel(block_ref, total_ref, out_ref):
    pass


def after(block, total):
    return pl.pallas_call(
        nothing_kernel,
        out_shape=jax.ShapeDtypeStruct(block.shape, block.dtype),
        in_specs=[ANY, ANY],
        out_specs=ANY,
        input_output_aliases={0: 0},
        compiler_params=pltpu.CompilerParams(vmem_limit_bytes=1 << 20),
        name="hand_on",
    )(block, total)


def moved(array, layers, peers, rule):
    pairs = []
    for layer in range(layers):
        for place in range(peers):
            target = rule(layer, place)
            if target is not None:
                pairs.append((layer * peers + place, target[0] * peers + target[1]))
    return lax.ppermute(array, AXES, pairs)


def resident_body(layers, peers, inverse_factor, coupling, forcing, upper_trace):
    chips = peers // 2

    def exchange(block, flip, shift):
        return moved(block, layers, peers, lambda layer, place: (layer ^ flip, place ^ shift))

    def arrive(vector, flip):
        if flip:
            order = [2, 0, 1] if chips == 4 else list(range(chips))
            direct = {chip: exchange(vector, flip, 2 * chip) for chip in order}
            if chips == 4:
                direct[3] = exchange(direct[2], 0, 2)
        else:
            direct = {chip: exchange(vector, 0, 2 * chip) if chip else vector for chip in range(chips - 1, -1, -1)}
            order = [0] + list(range(chips - 1, 0, -1))

        def across(chip):
            return exchange(direct[chip], 0, 1), 2 * chip + 1

        def own(chip):
            return direct[chip], 2 * chip

        if chips != 4:
            return [lambda total, chip=chip: [own(chip), across(chip)] for chip in order]
        if flip:

            def relayed(total):
                direct[3] = after(direct[3], total)
                return [own(3)]

            swapped = {chip: across(chip) for chip in order}
            return [
                lambda total: [own(2)],
                lambda total: [swapped[2], own(0)],
                lambda total: [swapped[0], own(1), swapped[1]],
                relayed,
                lambda total: [across(3)],
            ]
        swapped = {chip: across(chip) for chip in order}
        return [
            lambda total: [own(0), swapped[0], own(3)],
            lambda total: [swapped[3], own(2)],
            lambda total: [swapped[2], own(1)],
            lambda total: [swapped[1]],
        ]

    first, pack = first_vectors(forcing[0], coupling, upper_trace)
    groups = arrive(first, 0)
    gt = transposed(inverse_factor[0])
    below = moved(pack, layers, peers, lambda layer, place: (layer - 1, place) if layer else None)

    def apply(layer, groups, couple, kept, going_down, turning):
        total = None
        for group in groups[:-1]:
            pairs = group(total)
            total = partial_apply(layer, gt, [b for b, _ in pairs], [s for _, s in pairs], total)
        pairs = groups[-1](total)
        blocks, shifts = [b for b, _ in pairs], [s for _, s in pairs]
        return last_apply(layer, gt, blocks, shifts, total, couple, kept, going_down, turning)

    kept = first
    for layer in range(layers):
        turning = layer == layers - 1
        kept, sent = apply(layer, groups, coupling if turning else below, kept, True, turning)
        if layers > 1:
            groups = arrive(sent, layer ^ (layer - 1 if turning else layer + 1))
    for layer in range(layers - 2, -1, -1):
        kept, sent = apply(layer, groups, coupling, kept, False, False)
        if layer:
            groups = arrive(sent, layer ^ (layer - 1))
    return kept.reshape((1,) + forcing.shape[1:])


def solution(mesh):
    layers, peers = mesh.shape["depth"], mesh.shape["front"]
    placed = (
        P("depth", None, "front", None),
        P("depth", "front"),
        P("depth", None, None, "front"),
        P(None, None, "front"),
    )

    def body(inverse_factor, coupling, forcing, upper_trace):
        rows = inverse_factor.shape[2]
        fits = inverse_factor.size * 2 <= 40 << 20 and rows % WIDE == 0
        if fits and peers in (2, 4, 8) and layers in (2, 4, 8):
            return resident_body(layers, peers, inverse_factor, coupling, forcing, upper_trace)
        return plain_body(inverse_factor, coupling, forcing, upper_trace)

    return jax.shard_map(
        body, mesh=mesh, in_specs=placed, out_specs=P("depth", None, None, "front"), check_vma=False
    )
```

```python
import functools

import jax
import jax.numpy as jnp
from jax import lax
from jax.experimental import pallas as pl
from jax.experimental.pallas import tpu as pltpu
from jax.sharding import PartitionSpec as P

VMEM = pl.BlockSpec(memory_space=pltpu.VMEM)
ANY = pl.BlockSpec(memory_space=pl.ANY)
KERNEL_VMEM = 8 << 20
PRIORITY = 64
FILLER = pl.CostEstimate(flops=PRIORITY << 29, bytes_accessed=0, transcendentals=0)
AXES = ("depth", "front")


def passed_along(array, axis, by):
    peers = lax.axis_size(axis)
    pairs = [(i, i + by) for i in range(peers) if 0 <= i + by < peers]
    return lax.ppermute(array, axis, pairs)


def plain_body(inverse_factor, coupling, forcing, upper_trace):
    layer_index = lax.axis_index("depth")
    layer_count = lax.axis_size("depth")
    matrix = inverse_factor[0]
    couple = coupling[0]
    sources = forcing[0]

    def accumulate(segment):
        products = jnp.einsum("crk,dik->cdri", segment, matrix, preferred_element_type=jnp.float32)
        return jnp.stack([products[0, 0] - products[1, 1], products[1, 0] + products[0, 1]])

    downward = jnp.zeros_like(sources)
    outgoing = jnp.zeros_like(sources)
    for step in range(layer_count):
        incoming = upper_trace if step == 0 else passed_along(outgoing, "depth", 1)
        forced = (sources.astype(jnp.float32) - couple * incoming.astype(jnp.float32)).astype(jnp.bfloat16)
        outgoing = accumulate(lax.all_gather(forced, "front", axis=2, tiled=True)).astype(jnp.bfloat16)
        downward = jnp.where(layer_index == step, outgoing, downward)
    preconditioned = downward
    for step in range(layer_count - 2, -1, -1):
        scaled = (couple * preconditioned.astype(jnp.float32)).astype(jnp.bfloat16)
        incoming = passed_along(scaled, "depth", -1)
        correction = accumulate(lax.all_gather(incoming, "front", axis=2, tiled=True))
        updated = (downward.astype(jnp.float32) - correction).astype(jnp.bfloat16)
        preconditioned = jnp.where(layer_index == step, updated, preconditioned)
    return preconditioned[None]


def transpose_kernel(block, slots, g_ref, out_ref, held, sems):
    _, rows, depth = g_ref.shape
    per = depth // block
    count = 2 * per

    def copy(at, slot):
        part, col = at // per, lax.rem(at, per)
        window = pl.ds(pl.multiple_of(col * block, block), block)
        return pltpu.make_async_copy(g_ref.at[part, :, window], held.at[slot], sems.at[slot])

    for at in range(slots):
        copy(at, at).start()

    def turn(at, carry):
        slot = lax.rem(at, slots)
        copy(at, slot).wait()
        part, col = at // per, lax.rem(at, per)
        out_ref[part, pl.ds(pl.multiple_of(col * block, block), block), :] = held[slot].T

        @pl.when(at + slots < count)
        def _():
            copy(at + slots, slot).start()

        return carry

    lax.fori_loop(0, count, turn, 0)


def transposed(matrix):
    _, rows, depth = matrix.shape
    block, slots = 512, 6
    return pl.pallas_call(
        functools.partial(transpose_kernel, block, slots),
        out_shape=pltpu.VMEM((2, depth, rows), jnp.bfloat16),
        in_specs=[ANY],
        out_specs=VMEM,
        scratch_shapes=[pltpu.VMEM((slots, rows, block), jnp.bfloat16), pltpu.SemaphoreType.DMA((slots,))],
        compiler_params=pltpu.CompilerParams(vmem_limit_bytes=KERNEL_VMEM),
        cost_estimate=pl.CostEstimate(flops=PRIORITY * 100 * matrix.size, bytes_accessed=matrix.size * 2, transcendentals=0),
        name="transpose_factor",
    )(matrix)


def first_kernel(forcing_ref, couple_ref, trace_ref, forced_out, pack_out):
    r = forcing_ref.shape[1]
    couple = couple_ref[...]
    for c in range(2):
        rows = pl.ds(c * r, r)
        forcing = forcing_ref[c].astype(jnp.float32)
        forced_out[rows, :] = (forcing - couple * trace_ref[c].astype(jnp.float32)).astype(jnp.bfloat16)
        pack_out[rows, :] = forcing
    pack_out[2 * r :, :] = jnp.broadcast_to(couple, (8, couple.shape[1]))


def first_vectors(forcing, couple, trace):
    _, r, rows = forcing.shape
    return pl.pallas_call(
        first_kernel,
        out_shape=[
            jax.ShapeDtypeStruct((2 * r, rows), jnp.bfloat16),
            jax.ShapeDtypeStruct((2 * r + 8, rows), jnp.float32),
        ],
        in_specs=[VMEM] * 3,
        out_specs=[VMEM] * 2,
        compiler_params=pltpu.CompilerParams(vmem_limit_bytes=KERNEL_VMEM),
        name="first_forced",
    )(*[pltpu.with_memory_space_constraint(array, pltpu.HBM) for array in (forcing, couple, trace)])


def products(blocks, offsets, gt_ref, part, window):
    total = None
    for block, offset in zip(blocks, offsets, strict=True):
        depth = block.shape[1]
        columns = pl.ds(pl.multiple_of(offset * depth, depth), depth)
        term = jnp.dot(block[...], gt_ref[part, columns, window], preferred_element_type=jnp.float32)
        total = term if total is None else total + term
    return total


WIDE = 512


def partial_kernel(layer, shifts, resumed, gt_ref, *refs):
    blocks, refs = refs[: len(shifts)], refs[len(shifts) :]
    total_in = refs[0] if resumed else None
    total_out = refs[-1]
    rows = total_out.shape[2]

    @pl.when(lax.axis_index("depth") == layer)
    def _():
        me = lax.axis_index("front")
        offsets = [lax.bitwise_xor(me, jnp.int32(shift)) for shift in shifts]
        for part in range(2):
            for at in range(0, rows, WIDE):
                window = pl.ds(at, WIDE)
                value = products(blocks, offsets, gt_ref, part, window)
                total_out[part, :, window] = value if total_in is None else total_in[part, :, window] + value


def complex_of(blocks, offsets, gt_ref, total_ref, window):
    by_real = products(blocks, offsets, gt_ref, 0, window)
    by_imag = products(blocks, offsets, gt_ref, 1, window)
    if total_ref is not None:
        by_real += total_ref[0, :, window]
        by_imag += total_ref[1, :, window]
    r = by_real.shape[0] // 2
    return jnp.concatenate([by_real[:r] - by_imag[r:], by_real[r:] + by_imag[:r]], axis=0)


def last_kernel(layer, shifts, resumed, going_down, turning, gt_ref, *refs):
    blocks, refs = refs[: len(shifts)], refs[len(shifts) :]
    total_ref = refs[0] if resumed else None
    refs = refs[1:] if resumed else refs
    below = going_down and not turning
    final = not going_down and layer == 0
    couple_ref, kept_ref, result_out, *rest = refs if not going_down else (refs[0], None, *refs[1:])
    rows = result_out.shape[-1]

    def write(window, value):
        if final:
            r = value.shape[0] // 2
            for c in range(2):
                result_out[0, c, :, window] = value[c * r : (c + 1) * r]
        else:
            result_out[:, window] = value

    if final:

        @pl.when(lax.axis_index("depth") != layer)
        def _():
            write(slice(None), kept_ref[...])

    @pl.when(lax.axis_index("depth") == layer)
    def _():
        me = lax.axis_index("front")
        offsets = [lax.bitwise_xor(me, jnp.int32(shift)) for shift in shifts]
        for at in range(0, rows, WIDE):
            window = pl.ds(at, WIDE)
            value = complex_of(blocks, offsets, gt_ref, total_ref, window)
            r = value.shape[0]
            couple = couple_ref[r : r + 1, window] if below else couple_ref[:, window]
            if going_down:
                kept = value.astype(jnp.bfloat16)
                wide = couple * kept.astype(jnp.float32)
                sent = couple_ref[:r, window] - wide if below else wide
            else:
                kept = (kept_ref[:, window].astype(jnp.float32) - value).astype(jnp.bfloat16)
                sent = couple * kept.astype(jnp.float32)
            write(window, kept)
            if not final:
                rest[0][:, window] = sent.astype(jnp.bfloat16)


def keep_kernel(layer, gt_ref, kept_ref, result_ref, out_ref):
    mine = lax.axis_index("depth") == layer
    out_ref[...] = jnp.where(mine, result_ref[...], kept_ref[...])


def keep(layer, gt, kept, result):
    return pl.pallas_call(
        functools.partial(keep_kernel, layer),
        out_shape=jax.ShapeDtypeStruct(kept.shape, kept.dtype),
        in_specs=[ANY, VMEM, VMEM],
        out_specs=VMEM,
        compiler_params=pltpu.CompilerParams(vmem_limit_bytes=KERNEL_VMEM),
        cost_estimate=FILLER,
        name="keep",
    )(near(gt), kept, result)


def fetch_kernel(gt_ref, ref, result_ref, out_ref):
    out_ref[...] = ref[...]


def fetch(gt, array, result):
    return pl.pallas_call(
        fetch_kernel,
        out_shape=jax.ShapeDtypeStruct(array.shape, array.dtype),
        in_specs=[ANY, VMEM, ANY],
        out_specs=VMEM,
        compiler_params=pltpu.CompilerParams(vmem_limit_bytes=KERNEL_VMEM),
        cost_estimate=FILLER,
        name="fetch",
    )(near(gt), array, result)


def near(array):
    return pltpu.with_memory_space_constraint(array, pltpu.VMEM)


def cost(blocks, gt):
    depth = sum(block.shape[1] for block in blocks)
    rows = gt.shape[2]
    return pl.CostEstimate(
        flops=PRIORITY * 4 * blocks[0].shape[0] * depth * rows, bytes_accessed=4 * depth * rows, transcendentals=0
    )


def partial_apply(layer, gt, blocks, shifts, total):
    resumed = total is not None
    shape = (2, blocks[0].shape[0], gt.shape[2])
    operands = [gt, *blocks]
    aliases = {}
    if resumed:
        aliases = {len(operands): 0}
        operands.append(total)
    operands = [near(array) for array in operands]
    return pl.pallas_call(
        functools.partial(partial_kernel, layer, shifts, resumed),
        out_shape=pltpu.VMEM(shape, jnp.float32),
        in_specs=[VMEM] * len(operands),
        out_specs=VMEM,
        input_output_aliases=aliases,
        compiler_params=pltpu.CompilerParams(vmem_limit_bytes=KERNEL_VMEM),
        cost_estimate=cost(blocks, gt),
        name="partial_apply",
    )(*operands)


def last_apply(layer, gt, blocks, shifts, total, couple, kept, going_down, turning):
    resumed = total is not None
    operands = [gt, *blocks, *([total] if resumed else []), couple, *([] if going_down else [kept])]
    operands = [near(array) for array in operands]
    r, rows = blocks[0].shape[0], gt.shape[2]
    if going_down or layer:
        shapes = [jax.ShapeDtypeStruct((r, rows), jnp.bfloat16)] * 2
    else:
        shapes = [jax.ShapeDtypeStruct((1, 2, r // 2, rows), jnp.bfloat16)]
    return pl.pallas_call(
        functools.partial(last_kernel, layer, shifts, resumed, going_down, turning),
        out_shape=shapes,
        in_specs=[VMEM] * len(operands),
        out_specs=[VMEM] * len(shapes),
        compiler_params=pltpu.CompilerParams(vmem_limit_bytes=KERNEL_VMEM),
        cost_estimate=cost(blocks, gt),
        name="last_apply",
    )(*operands)


def nothing_kernel(block_ref, total_ref, out_ref):
    pass


def after(block, total):
    return pl.pallas_call(
        nothing_kernel,
        out_shape=jax.ShapeDtypeStruct(block.shape, block.dtype),
        in_specs=[ANY, ANY],
        out_specs=ANY,
        input_output_aliases={0: 0},
        compiler_params=pltpu.CompilerParams(vmem_limit_bytes=1 << 20),
        name="hand_on",
    )(block, total)


def moved(array, layers, peers, rule):
    pairs = []
    for layer in range(layers):
        for place in range(peers):
            target = rule(layer, place)
            if target is not None:
                pairs.append((layer * peers + place, target[0] * peers + target[1]))
    return lax.ppermute(array, AXES, pairs)


def resident_body(layers, peers, inverse_factor, coupling, forcing, upper_trace):
    chips = peers // 2

    def exchange(block, flip, shift):
        return moved(block, layers, peers, lambda layer, place: (layer ^ flip, place ^ shift))

    def arrive(vector, flip):
        if flip:
            order = [2, 0, 1] if chips == 4 else list(range(chips))
            direct = {chip: exchange(vector, flip, 2 * chip) for chip in order}
            if chips == 4:
                direct[3] = exchange(direct[2], 0, 2)
        else:
            direct = {chip: exchange(vector, 0, 2 * chip) if chip else vector for chip in range(chips - 1, -1, -1)}
            order = [0] + list(range(chips - 1, 0, -1))

        def across(chip):
            return exchange(direct[chip], 0, 1), 2 * chip + 1

        def own(chip):
            return direct[chip], 2 * chip

        if chips != 4:
            return [lambda total, chip=chip: [own(chip), across(chip)] for chip in order]
        if flip:

            swapped = {2: across(2)}

            def held(chip, total):
                direct[chip] = after(direct[chip], total)
                swapped[chip] = across(chip)
                return own(chip)

            return [
                lambda total: [own(2)],
                lambda total: [swapped[2]],
                lambda total: [held(0, total), held(1, total)],
                lambda total: [swapped[0], swapped[1]],
                lambda total: [held(3, total)],
                lambda total: [swapped[3]],
            ]
        swapped = {chip: across(chip) for chip in order}
        return [
            lambda total: [own(0), swapped[0], own(3)],
            lambda total: [swapped[3], own(2)],
            lambda total: [swapped[2], own(1)],
            lambda total: [swapped[1]],
        ]

    first, pack = first_vectors(forcing[0], coupling, upper_trace)
    groups = arrive(first, 0)
    gt = transposed(inverse_factor[0])
    below = moved(pack, layers, peers, lambda layer, place: (layer - 1, place) if layer else None)

    def apply(layer, groups, couple, kept, going_down, turning):
        total = None
        for group in groups[:-1]:
            pairs = group(total)
            total = partial_apply(layer, gt, [b for b, _ in pairs], [s for _, s in pairs], total)
        pairs = groups[-1](total)
        blocks, shifts = [b for b, _ in pairs], [s for _, s in pairs]
        return last_apply(layer, gt, blocks, shifts, total, couple, kept, going_down, turning)

    kept = result = None
    for layer in range(layers):
        turning = layer == layers - 1
        if layer:
            kept = result if layer == 1 else keep(layer - 1, gt, kept, result)
        couple = coupling if turning else fetch(gt, below, result if layer else first)
        result, sent = apply(layer, groups, couple, kept, True, turning)
        groups = arrive(sent, layer ^ (layer - 1 if turning else layer + 1))
    for layer in range(layers - 2, -1, -1):
        kept = keep(layer + 1, gt, kept, result)
        result, *sent = apply(layer, groups, coupling, kept, False, False)
        if layer:
            groups = arrive(sent[0], layer ^ (layer - 1))
    return result


def solution(mesh):
    layers, peers = mesh.shape["depth"], mesh.shape["front"]
    placed = (
        P("depth", None, "front", None),
        P("depth", "front"),
        P("depth", None, None, "front"),
        P(None, None, "front"),
    )

    def body(inverse_factor, coupling, forcing, upper_trace):
        rows = inverse_factor.shape[2]
        fits = inverse_factor.size * 2 <= 40 << 20 and rows % WIDE == 0
        if fits and peers in (2, 4, 8) and layers in (2, 4, 8):
            return resident_body(layers, peers, inverse_factor, coupling, forcing, upper_trace)
        return plain_body(inverse_factor, coupling, forcing, upper_trace)

    return jax.shard_map(
        body, mesh=mesh, in_specs=placed, out_specs=P("depth", None, None, "front"), check_vma=False
    )
```

```python
import functools

import jax
import jax.numpy as jnp
from jax import lax
from jax.experimental import pallas as pl
from jax.experimental.pallas import tpu as pltpu
from jax.sharding import PartitionSpec as P

VMEM = pl.BlockSpec(memory_space=pltpu.VMEM)
ANY = pl.BlockSpec(memory_space=pl.ANY)
KERNEL_VMEM = 8 << 20
PRIORITY = 64
FILLER = pl.CostEstimate(flops=PRIORITY << 29, bytes_accessed=0, transcendentals=0)
AXES = ("depth", "front")


def passed_along(array, axis, by):
    peers = lax.axis_size(axis)
    pairs = [(i, i + by) for i in range(peers) if 0 <= i + by < peers]
    return lax.ppermute(array, axis, pairs)


def plain_body(inverse_factor, coupling, forcing, upper_trace):
    layer_index = lax.axis_index("depth")
    layer_count = lax.axis_size("depth")
    matrix = inverse_factor[0]
    couple = coupling[0]
    sources = forcing[0]

    def accumulate(segment):
        products = jnp.einsum("crk,dik->cdri", segment, matrix, preferred_element_type=jnp.float32)
        return jnp.stack([products[0, 0] - products[1, 1], products[1, 0] + products[0, 1]])

    downward = jnp.zeros_like(sources)
    outgoing = jnp.zeros_like(sources)
    for step in range(layer_count):
        incoming = upper_trace if step == 0 else passed_along(outgoing, "depth", 1)
        forced = (sources.astype(jnp.float32) - couple * incoming.astype(jnp.float32)).astype(jnp.bfloat16)
        outgoing = accumulate(lax.all_gather(forced, "front", axis=2, tiled=True)).astype(jnp.bfloat16)
        downward = jnp.where(layer_index == step, outgoing, downward)
    preconditioned = downward
    for step in range(layer_count - 2, -1, -1):
        scaled = (couple * preconditioned.astype(jnp.float32)).astype(jnp.bfloat16)
        incoming = passed_along(scaled, "depth", -1)
        correction = accumulate(lax.all_gather(incoming, "front", axis=2, tiled=True))
        updated = (downward.astype(jnp.float32) - correction).astype(jnp.bfloat16)
        preconditioned = jnp.where(layer_index == step, updated, preconditioned)
    return preconditioned[None]


def transpose_kernel(block, slots, g_ref, out_ref, held, sems):
    _, rows, depth = g_ref.shape
    per = depth // block
    count = 2 * per

    def copy(at, slot):
        part, col = at // per, lax.rem(at, per)
        window = pl.ds(pl.multiple_of(col * block, block), block)
        return pltpu.make_async_copy(g_ref.at[part, :, window], held.at[slot], sems.at[slot])

    for at in range(slots):
        copy(at, at).start()

    def turn(at, carry):
        slot = lax.rem(at, slots)
        copy(at, slot).wait()
        part, col = at // per, lax.rem(at, per)
        out_ref[part, pl.ds(pl.multiple_of(col * block, block), block), :] = held[slot].T

        @pl.when(at + slots < count)
        def _():
            copy(at + slots, slot).start()

        return carry

    lax.fori_loop(0, count, turn, 0)


def transposed(matrix):
    _, rows, depth = matrix.shape
    block, slots = 512, 6
    return pl.pallas_call(
        functools.partial(transpose_kernel, block, slots),
        out_shape=pltpu.VMEM((2, depth, rows), jnp.bfloat16),
        in_specs=[ANY],
        out_specs=VMEM,
        scratch_shapes=[pltpu.VMEM((slots, rows, block), jnp.bfloat16), pltpu.SemaphoreType.DMA((slots,))],
        compiler_params=pltpu.CompilerParams(vmem_limit_bytes=KERNEL_VMEM),
        cost_estimate=pl.CostEstimate(flops=PRIORITY * 100 * matrix.size, bytes_accessed=matrix.size * 2, transcendentals=0),
        name="transpose_factor",
    )(matrix)


def first_kernel(forcing_ref, couple_ref, trace_ref, forced_out, pack_out):
    r = forcing_ref.shape[1]
    couple = couple_ref[...]
    for c in range(2):
        rows = pl.ds(c * r, r)
        forcing = forcing_ref[c].astype(jnp.float32)
        forced_out[rows, :] = (forcing - couple * trace_ref[c].astype(jnp.float32)).astype(jnp.bfloat16)
        pack_out[rows, :] = forcing
    pack_out[2 * r :, :] = jnp.broadcast_to(couple, (8, couple.shape[1]))


def first_vectors(forcing, couple, trace):
    _, r, rows = forcing.shape
    return pl.pallas_call(
        first_kernel,
        out_shape=[
            jax.ShapeDtypeStruct((2 * r, rows), jnp.bfloat16),
            jax.ShapeDtypeStruct((2 * r + 8, rows), jnp.float32),
        ],
        in_specs=[VMEM] * 3,
        out_specs=[VMEM] * 2,
        compiler_params=pltpu.CompilerParams(vmem_limit_bytes=KERNEL_VMEM),
        name="first_forced",
    )(*[pltpu.with_memory_space_constraint(array, pltpu.HBM) for array in (forcing, couple, trace)])


def products(blocks, offsets, gt_ref, part, window):
    total = None
    for block, offset in zip(blocks, offsets, strict=True):
        depth = block.shape[1]
        columns = pl.ds(pl.multiple_of(offset * depth, depth), depth)
        term = jnp.dot(block[...], gt_ref[part, columns, window], preferred_element_type=jnp.float32)
        total = term if total is None else total + term
    return total


WIDE = 512


def partial_kernel(layer, shifts, resumed, gt_ref, *refs):
    blocks, refs = refs[: len(shifts)], refs[len(shifts) :]
    total_in = refs[0] if resumed else None
    total_out = refs[-1]
    rows = total_out.shape[2]

    @pl.when(lax.axis_index("depth") == layer)
    def _():
        me = lax.axis_index("front")
        offsets = [lax.bitwise_xor(me, jnp.int32(shift)) for shift in shifts]
        for part in range(2):
            for at in range(0, rows, WIDE):
                window = pl.ds(at, WIDE)
                value = products(blocks, offsets, gt_ref, part, window)
                total_out[part, :, window] = value if total_in is None else total_in[part, :, window] + value


def complex_of(blocks, offsets, gt_ref, total_ref, window):
    by_real = products(blocks, offsets, gt_ref, 0, window)
    by_imag = products(blocks, offsets, gt_ref, 1, window)
    if total_ref is not None:
        by_real += total_ref[0, :, window]
        by_imag += total_ref[1, :, window]
    r = by_real.shape[0] // 2
    return jnp.concatenate([by_real[:r] - by_imag[r:], by_real[r:] + by_imag[:r]], axis=0)


def last_kernel(layer, shifts, resumed, going_down, turning, gt_ref, *refs):
    blocks, refs = refs[: len(shifts)], refs[len(shifts) :]
    total_ref = refs[0] if resumed else None
    refs = refs[1:] if resumed else refs
    below = going_down and not turning
    final = not going_down and layer == 0
    couple_ref, kept_ref, result_out, *rest = refs if not going_down else (refs[0], None, *refs[1:])
    rows = result_out.shape[-1]

    def write(window, value):
        if final:
            r = value.shape[0] // 2
            for c in range(2):
                result_out[0, c, :, window] = value[c * r : (c + 1) * r]
        else:
            result_out[:, window] = value

    if final:

        @pl.when(lax.axis_index("depth") != layer)
        def _():
            write(slice(None), kept_ref[...])

    @pl.when(lax.axis_index("depth") == layer)
    def _():
        me = lax.axis_index("front")
        offsets = [lax.bitwise_xor(me, jnp.int32(shift)) for shift in shifts]
        for at in range(0, rows, WIDE):
            window = pl.ds(at, WIDE)
            value = complex_of(blocks, offsets, gt_ref, total_ref, window)
            r = value.shape[0]
            couple = couple_ref[r : r + 1, window] if below else couple_ref[:, window]
            if going_down:
                kept = value.astype(jnp.bfloat16)
                wide = couple * kept.astype(jnp.float32)
                sent = couple_ref[:r, window] - wide if below else wide
            else:
                kept = (kept_ref[:, window].astype(jnp.float32) - value).astype(jnp.bfloat16)
                sent = couple * kept.astype(jnp.float32)
            write(window, kept)
            if not final:
                rest[0][:, window] = sent.astype(jnp.bfloat16)


def keep_kernel(layer, gt_ref, kept_ref, result_ref, out_ref):
    mine = lax.axis_index("depth") == layer
    out_ref[...] = jnp.where(mine, result_ref[...], kept_ref[...])


def keep(layer, gt, kept, result):
    return pl.pallas_call(
        functools.partial(keep_kernel, layer),
        out_shape=jax.ShapeDtypeStruct(kept.shape, kept.dtype),
        in_specs=[ANY, VMEM, VMEM],
        out_specs=VMEM,
        compiler_params=pltpu.CompilerParams(vmem_limit_bytes=KERNEL_VMEM),
        cost_estimate=FILLER,
        name="keep",
    )(near(gt), kept, result)


def fetch_kernel(gt_ref, ref, result_ref, out_ref):
    out_ref[...] = ref[...]


def fetch(gt, array, result):
    return pl.pallas_call(
        fetch_kernel,
        out_shape=jax.ShapeDtypeStruct(array.shape, array.dtype),
        in_specs=[ANY, VMEM, ANY],
        out_specs=VMEM,
        compiler_params=pltpu.CompilerParams(vmem_limit_bytes=KERNEL_VMEM),
        cost_estimate=FILLER,
        name="fetch",
    )(near(gt), array, result)


def near(array):
    return pltpu.with_memory_space_constraint(array, pltpu.VMEM)


def cost(blocks, gt):
    depth = sum(block.shape[1] for block in blocks)
    rows = gt.shape[2]
    return pl.CostEstimate(
        flops=PRIORITY * 4 * blocks[0].shape[0] * depth * rows, bytes_accessed=4 * depth * rows, transcendentals=0
    )


def partial_apply(layer, gt, blocks, shifts, total):
    resumed = total is not None
    shape = (2, blocks[0].shape[0], gt.shape[2])
    operands = [gt, *blocks]
    aliases = {}
    if resumed:
        aliases = {len(operands): 0}
        operands.append(total)
    operands = [near(array) for array in operands]
    return pl.pallas_call(
        functools.partial(partial_kernel, layer, shifts, resumed),
        out_shape=pltpu.VMEM(shape, jnp.float32),
        in_specs=[VMEM] * len(operands),
        out_specs=VMEM,
        input_output_aliases=aliases,
        compiler_params=pltpu.CompilerParams(vmem_limit_bytes=KERNEL_VMEM),
        cost_estimate=cost(blocks, gt),
        name="partial_apply",
    )(*operands)


def last_apply(layer, gt, blocks, shifts, total, couple, kept, going_down, turning):
    resumed = total is not None
    operands = [gt, *blocks, *([total] if resumed else []), couple, *([] if going_down else [kept])]
    operands = [near(array) for array in operands]
    r, rows = blocks[0].shape[0], gt.shape[2]
    if going_down or layer:
        shapes = [jax.ShapeDtypeStruct((r, rows), jnp.bfloat16)] * 2
    else:
        shapes = [jax.ShapeDtypeStruct((1, 2, r // 2, rows), jnp.bfloat16)]
    return pl.pallas_call(
        functools.partial(last_kernel, layer, shifts, resumed, going_down, turning),
        out_shape=shapes,
        in_specs=[VMEM] * len(operands),
        out_specs=[VMEM] * len(shapes),
        compiler_params=pltpu.CompilerParams(vmem_limit_bytes=KERNEL_VMEM),
        cost_estimate=cost(blocks, gt),
        name="last_apply",
    )(*operands)


def nothing_kernel(block_ref, total_ref, out_ref):
    pass


def after(block, total):
    return pl.pallas_call(
        nothing_kernel,
        out_shape=jax.ShapeDtypeStruct(block.shape, block.dtype),
        in_specs=[ANY, ANY],
        out_specs=ANY,
        input_output_aliases={0: 0},
        compiler_params=pltpu.CompilerParams(vmem_limit_bytes=1 << 20),
        name="hand_on",
    )(block, total)


def moved(array, layers, peers, rule):
    pairs = []
    for layer in range(layers):
        for place in range(peers):
            target = rule(layer, place)
            if target is not None:
                pairs.append((layer * peers + place, target[0] * peers + target[1]))
    return lax.ppermute(array, AXES, pairs)


def resident_body(layers, peers, inverse_factor, coupling, forcing, upper_trace):
    chips = peers // 2

    def exchange(block, flip, shift):
        return moved(block, layers, peers, lambda layer, place: (layer ^ flip, place ^ shift))

    def arrive(vector, flip):
        if flip:
            order = [2, 0, 1] if chips == 4 else list(range(chips))
            direct = {chip: exchange(vector, flip, 2 * chip) for chip in order}
            if chips == 4:
                direct[3] = exchange(direct[2], 0, 2)
        else:
            direct = {chip: exchange(vector, 0, 2 * chip) if chip else vector for chip in range(chips - 1, -1, -1)}
            order = [0] + list(range(chips - 1, 0, -1))

        def across(chip):
            return exchange(direct[chip], 0, 1), 2 * chip + 1

        def own(chip):
            return direct[chip], 2 * chip

        def held(chip, total):
            if total is not None:
                direct[chip] = after(direct[chip], total)
            swapped[chip] = across(chip)
            return own(chip)

        if chips != 4:
            return [lambda total, chip=chip: [own(chip), across(chip)] for chip in order]
        swapped = {order[0]: across(order[0])}
        if flip:
            return [
                lambda total: [own(2)],
                lambda total: [swapped[2]],
                lambda total: [held(0, total), held(1, total)],
                lambda total: [held(3, total), swapped[0], swapped[1]],
                lambda total: [swapped[3]],
            ]
        return [
            lambda total: [own(0), swapped[0]],
            lambda total: [held(3, total), held(2, total)],
            lambda total: [held(1, total), swapped[3]],
            lambda total: [swapped[2]],
            lambda total: [swapped[1]],
        ]

    first, pack = first_vectors(forcing[0], coupling, upper_trace)
    groups = arrive(first, 0)
    gt = transposed(inverse_factor[0])
    below = moved(pack, layers, peers, lambda layer, place: (layer - 1, place) if layer else None)

    def apply(layer, groups, couple, kept, going_down, turning):
        total = None
        for group in groups[:-1]:
            pairs = group(total)
            total = partial_apply(layer, gt, [b for b, _ in pairs], [s for _, s in pairs], total)
        pairs = groups[-1](total)
        blocks, shifts = [b for b, _ in pairs], [s for _, s in pairs]
        return last_apply(layer, gt, blocks, shifts, total, couple, kept, going_down, turning)

    kept = result = None
    for layer in range(layers):
        turning = layer == layers - 1
        if layer:
            kept = result if layer == 1 else keep(layer - 1, gt, kept, result)
        couple = coupling if turning else fetch(gt, below, result if layer else first)
        result, sent = apply(layer, groups, couple, kept, True, turning)
        groups = arrive(sent, layer ^ (layer - 1 if turning else layer + 1))
    for layer in range(layers - 2, -1, -1):
        kept = keep(layer + 1, gt, kept, result)
        result, *sent = apply(layer, groups, coupling, kept, False, False)
        if layer:
            groups = arrive(sent[0], layer ^ (layer - 1))
    return result


def solution(mesh):
    layers, peers = mesh.shape["depth"], mesh.shape["front"]
    placed = (
        P("depth", None, "front", None),
        P("depth", "front"),
        P("depth", None, None, "front"),
        P(None, None, "front"),
    )

    def body(inverse_factor, coupling, forcing, upper_trace):
        rows = inverse_factor.shape[2]
        fits = inverse_factor.size * 2 <= 40 << 20 and rows % WIDE == 0
        if fits and peers in (2, 4, 8) and layers in (2, 4, 8):
            return resident_body(layers, peers, inverse_factor, coupling, forcing, upper_trace)
        return plain_body(inverse_factor, coupling, forcing, upper_trace)

    return jax.shard_map(
        body, mesh=mesh, in_specs=placed, out_specs=P("depth", None, None, "front"), check_vma=False
    )
```

```python
import functools

import jax
import jax.numpy as jnp
from jax import lax
from jax.experimental import pallas as pl
from jax.experimental.pallas import tpu as pltpu
from jax.sharding import PartitionSpec as P

VMEM = pl.BlockSpec(memory_space=pltpu.VMEM)
ANY = pl.BlockSpec(memory_space=pl.ANY)
KERNEL_VMEM = 8 << 20
PRIORITY = 64
FILLER = pl.CostEstimate(flops=PRIORITY << 29, bytes_accessed=0, transcendentals=0)
AXES = ("depth", "front")


def passed_along(array, axis, by):
    peers = lax.axis_size(axis)
    pairs = [(i, i + by) for i in range(peers) if 0 <= i + by < peers]
    return lax.ppermute(array, axis, pairs)


def plain_body(inverse_factor, coupling, forcing, upper_trace):
    layer_index = lax.axis_index("depth")
    layer_count = lax.axis_size("depth")
    matrix = inverse_factor[0]
    couple = coupling[0]
    sources = forcing[0]

    def accumulate(segment):
        products = jnp.einsum("crk,dik->cdri", segment, matrix, preferred_element_type=jnp.float32)
        return jnp.stack([products[0, 0] - products[1, 1], products[1, 0] + products[0, 1]])

    downward = jnp.zeros_like(sources)
    outgoing = jnp.zeros_like(sources)
    for step in range(layer_count):
        incoming = upper_trace if step == 0 else passed_along(outgoing, "depth", 1)
        forced = (sources.astype(jnp.float32) - couple * incoming.astype(jnp.float32)).astype(jnp.bfloat16)
        outgoing = accumulate(lax.all_gather(forced, "front", axis=2, tiled=True)).astype(jnp.bfloat16)
        downward = jnp.where(layer_index == step, outgoing, downward)
    preconditioned = downward
    for step in range(layer_count - 2, -1, -1):
        scaled = (couple * preconditioned.astype(jnp.float32)).astype(jnp.bfloat16)
        incoming = passed_along(scaled, "depth", -1)
        correction = accumulate(lax.all_gather(incoming, "front", axis=2, tiled=True))
        updated = (downward.astype(jnp.float32) - correction).astype(jnp.bfloat16)
        preconditioned = jnp.where(layer_index == step, updated, preconditioned)
    return preconditioned[None]


def transpose_kernel(block, slots, g_ref, out_ref, held, sems):
    _, rows, depth = g_ref.shape
    per = depth // block
    count = 2 * per

    def copy(at, slot):
        part, col = at // per, lax.rem(at, per)
        window = pl.ds(pl.multiple_of(col * block, block), block)
        return pltpu.make_async_copy(g_ref.at[part, :, window], held.at[slot], sems.at[slot])

    for at in range(slots):
        copy(at, at).start()

    def turn(at, carry):
        slot = lax.rem(at, slots)
        copy(at, slot).wait()
        part, col = at // per, lax.rem(at, per)
        out_ref[part, pl.ds(pl.multiple_of(col * block, block), block), :] = held[slot].T

        @pl.when(at + slots < count)
        def _():
            copy(at + slots, slot).start()

        return carry

    lax.fori_loop(0, count, turn, 0)


def transposed(matrix):
    _, rows, depth = matrix.shape
    block, slots = 512, 6
    return pl.pallas_call(
        functools.partial(transpose_kernel, block, slots),
        out_shape=pltpu.VMEM((2, depth, rows), jnp.bfloat16),
        in_specs=[ANY],
        out_specs=VMEM,
        scratch_shapes=[pltpu.VMEM((slots, rows, block), jnp.bfloat16), pltpu.SemaphoreType.DMA((slots,))],
        compiler_params=pltpu.CompilerParams(vmem_limit_bytes=KERNEL_VMEM),
        cost_estimate=pl.CostEstimate(flops=PRIORITY * 100 * matrix.size, bytes_accessed=matrix.size * 2, transcendentals=0),
        name="transpose_factor",
    )(matrix)


def first_kernel(forcing_ref, couple_ref, trace_ref, forced_out, pack_out):
    r = forcing_ref.shape[1]
    couple = couple_ref[...]
    for c in range(2):
        rows = pl.ds(c * r, r)
        forcing = forcing_ref[c].astype(jnp.float32)
        forced_out[rows, :] = (forcing - couple * trace_ref[c].astype(jnp.float32)).astype(jnp.bfloat16)
        pack_out[rows, :] = forcing
    pack_out[2 * r :, :] = jnp.broadcast_to(couple, (8, couple.shape[1]))


def first_vectors(forcing, couple, trace):
    _, r, rows = forcing.shape
    return pl.pallas_call(
        first_kernel,
        out_shape=[
            jax.ShapeDtypeStruct((2 * r, rows), jnp.bfloat16),
            jax.ShapeDtypeStruct((2 * r + 8, rows), jnp.float32),
        ],
        in_specs=[VMEM] * 3,
        out_specs=[VMEM] * 2,
        compiler_params=pltpu.CompilerParams(vmem_limit_bytes=KERNEL_VMEM),
        name="first_forced",
    )(*[pltpu.with_memory_space_constraint(array, pltpu.HBM) for array in (forcing, couple, trace)])


def products(blocks, offsets, gt_ref, part, window):
    total = None
    for block, offset in zip(blocks, offsets, strict=True):
        depth = block.shape[1]
        columns = pl.ds(pl.multiple_of(offset * depth, depth), depth)
        term = jnp.dot(block[...], gt_ref[part, columns, window], preferred_element_type=jnp.float32)
        total = term if total is None else total + term
    return total


WIDE = 512


def partial_kernel(layer, shifts, resumed, gt_ref, *refs):
    blocks, refs = refs[: len(shifts)], refs[len(shifts) :]
    total_in = refs[0] if resumed else None
    total_out = refs[-1]
    rows = total_out.shape[2]

    @pl.when(lax.axis_index("depth") == layer)
    def _():
        me = lax.axis_index("front")
        offsets = [lax.bitwise_xor(me, jnp.int32(shift)) for shift in shifts]
        for part in range(2):
            for at in range(0, rows, WIDE):
                window = pl.ds(at, WIDE)
                value = products(blocks, offsets, gt_ref, part, window)
                total_out[part, :, window] = value if total_in is None else total_in[part, :, window] + value


def complex_of(blocks, offsets, gt_ref, total_ref, window):
    by_real = products(blocks, offsets, gt_ref, 0, window)
    by_imag = products(blocks, offsets, gt_ref, 1, window)
    if total_ref is not None:
        by_real += total_ref[0, :, window]
        by_imag += total_ref[1, :, window]
    r = by_real.shape[0] // 2
    return jnp.concatenate([by_real[:r] - by_imag[r:], by_real[r:] + by_imag[:r]], axis=0)


def last_kernel(layer, shifts, resumed, going_down, turning, gt_ref, *refs):
    blocks, refs = refs[: len(shifts)], refs[len(shifts) :]
    total_ref = refs[0] if resumed else None
    refs = refs[1:] if resumed else refs
    below = going_down and not turning
    final = not going_down and layer == 0
    couple_ref, kept_ref, result_out, *rest = refs if not going_down else (refs[0], None, *refs[1:])
    rows = result_out.shape[-1]
    lazy = below and layer == 0

    def write(window, value):
        if final:
            r = value.shape[0] // 2
            for c in range(2):
                result_out[0, c, :, window] = value[c * r : (c + 1) * r]
        else:
            result_out[:, window] = value

    if final:

        @pl.when(lax.axis_index("depth") != layer)
        def _():
            write(slice(None), kept_ref[...])

    @pl.when(lax.axis_index("depth") == layer)
    def _():
        me = lax.axis_index("front")
        offsets = [lax.bitwise_xor(me, jnp.int32(shift)) for shift in shifts]
        source_ref = couple_ref
        if lazy:
            source_ref, sem = rest[1:]
            copy = pltpu.make_async_copy(couple_ref, source_ref, sem)
            copy.start()
        windows = [pl.ds(at, WIDE) for at in range(0, rows, WIDE)]
        values = [complex_of(blocks, offsets, gt_ref, total_ref, window) for window in windows]
        if lazy:
            copy.wait()
        for window, value in zip(windows, values, strict=True):
            r = value.shape[0]
            couple = source_ref[r : r + 1, window] if below else source_ref[:, window]
            if going_down:
                kept = value.astype(jnp.bfloat16)
                wide = couple * kept.astype(jnp.float32)
                sent = source_ref[:r, window] - wide if below else wide
            else:
                kept = (kept_ref[:, window].astype(jnp.float32) - value).astype(jnp.bfloat16)
                sent = couple * kept.astype(jnp.float32)
            write(window, kept)
            if not final:
                rest[0][:, window] = sent.astype(jnp.bfloat16)


def keep_kernel(layer, gt_ref, kept_ref, result_ref, out_ref):
    mine = lax.axis_index("depth") == layer
    out_ref[...] = jnp.where(mine, result_ref[...], kept_ref[...])


def keep(layer, gt, kept, result):
    return pl.pallas_call(
        functools.partial(keep_kernel, layer),
        out_shape=jax.ShapeDtypeStruct(kept.shape, kept.dtype),
        in_specs=[ANY, VMEM, VMEM],
        out_specs=VMEM,
        compiler_params=pltpu.CompilerParams(vmem_limit_bytes=KERNEL_VMEM),
        cost_estimate=FILLER,
        name="keep",
    )(near(gt), kept, result)


def fetch_kernel(gt_ref, ref, result_ref, out_ref):
    out_ref[...] = ref[...]


def fetch(gt, array, result):
    return pl.pallas_call(
        fetch_kernel,
        out_shape=jax.ShapeDtypeStruct(array.shape, array.dtype),
        in_specs=[ANY, VMEM, ANY],
        out_specs=VMEM,
        compiler_params=pltpu.CompilerParams(vmem_limit_bytes=KERNEL_VMEM),
        cost_estimate=FILLER,
        name="fetch",
    )(near(gt), array, result)


def near(array):
    return pltpu.with_memory_space_constraint(array, pltpu.VMEM)


def cost(blocks, gt):
    depth = sum(block.shape[1] for block in blocks)
    rows = gt.shape[2]
    return pl.CostEstimate(
        flops=PRIORITY * 4 * blocks[0].shape[0] * depth * rows, bytes_accessed=4 * depth * rows, transcendentals=0
    )


def partial_apply(layer, gt, blocks, shifts, total):
    resumed = total is not None
    shape = (2, blocks[0].shape[0], gt.shape[2])
    operands = [gt, *blocks]
    aliases = {}
    if resumed:
        aliases = {len(operands): 0}
        operands.append(total)
    operands = [near(array) for array in operands]
    return pl.pallas_call(
        functools.partial(partial_kernel, layer, shifts, resumed),
        out_shape=pltpu.VMEM(shape, jnp.float32),
        in_specs=[VMEM] * len(operands),
        out_specs=VMEM,
        input_output_aliases=aliases,
        compiler_params=pltpu.CompilerParams(vmem_limit_bytes=KERNEL_VMEM),
        cost_estimate=cost(blocks, gt),
        name="partial_apply",
    )(*operands)


def last_apply(layer, gt, blocks, shifts, total, couple, kept, going_down, turning):
    resumed = total is not None
    operands = [gt, *blocks, *([total] if resumed else []), couple, *([] if going_down else [kept])]
    lazy = going_down and not turning and layer == 0
    operands = [array if lazy and array is couple else near(array) for array in operands]
    specs = [VMEM] * len(operands)
    if lazy:
        specs[-1] = ANY
    r, rows = blocks[0].shape[0], gt.shape[2]
    if going_down or layer:
        shapes = [jax.ShapeDtypeStruct((r, rows), jnp.bfloat16)] * 2
    else:
        shapes = [jax.ShapeDtypeStruct((1, 2, r // 2, rows), jnp.bfloat16)]
    return pl.pallas_call(
        functools.partial(last_kernel, layer, shifts, resumed, going_down, turning),
        out_shape=shapes,
        in_specs=specs,
        out_specs=[VMEM] * len(shapes),
        scratch_shapes=[pltpu.VMEM(couple.shape, couple.dtype), pltpu.SemaphoreType.DMA] if lazy else [],
        compiler_params=pltpu.CompilerParams(vmem_limit_bytes=KERNEL_VMEM),
        cost_estimate=cost(blocks, gt),
        name="last_apply",
    )(*operands)


def nothing_kernel(block_ref, total_ref, out_ref):
    pass


def after(block, total):
    return pl.pallas_call(
        nothing_kernel,
        out_shape=jax.ShapeDtypeStruct(block.shape, block.dtype),
        in_specs=[ANY, ANY],
        out_specs=ANY,
        input_output_aliases={0: 0},
        compiler_params=pltpu.CompilerParams(vmem_limit_bytes=1 << 20),
        name="hand_on",
    )(block, total)


def moved(array, layers, peers, rule):
    pairs = []
    for layer in range(layers):
        for place in range(peers):
            target = rule(layer, place)
            if target is not None:
                pairs.append((layer * peers + place, target[0] * peers + target[1]))
    return lax.ppermute(array, AXES, pairs)


def resident_body(layers, peers, inverse_factor, coupling, forcing, upper_trace):
    chips = peers // 2

    def exchange(block, flip, shift):
        return moved(block, layers, peers, lambda layer, place: (layer ^ flip, place ^ shift))

    def arrive(vector, flip):
        if flip:
            order = [2, 0, 1] if chips == 4 else list(range(chips))
            direct = {chip: exchange(vector, flip, 2 * chip) for chip in order}
            if chips == 4:
                direct[3] = exchange(direct[2], 0, 2)
        else:
            direct = {chip: exchange(vector, 0, 2 * chip) if chip else vector for chip in range(chips - 1, -1, -1)}
            order = [0] + list(range(chips - 1, 0, -1))

        def across(chip):
            return exchange(direct[chip], 0, 1), 2 * chip + 1

        def own(chip):
            return direct[chip], 2 * chip

        def held(chip, total):
            if total is not None:
                direct[chip] = after(direct[chip], total)
            swapped[chip] = across(chip)
            return own(chip)

        if chips != 4:
            return [lambda total, chip=chip: [own(chip), across(chip)] for chip in order]
        swapped = {order[0]: across(order[0])}
        if flip:
            return [
                lambda total: [own(2)],
                lambda total: [swapped[2]],
                lambda total: [held(0, total), held(1, total)],
                lambda total: [held(3, total), swapped[0], swapped[1]],
                lambda total: [swapped[3]],
            ]
        return [
            lambda total: [own(0), swapped[0]],
            lambda total: [held(3, total), held(2, total), held(1, total)],
            lambda total: [swapped[3], swapped[2], swapped[1]],
        ]

    first, pack = first_vectors(forcing[0], coupling, upper_trace)
    groups = arrive(first, 0)
    gt = transposed(inverse_factor[0])
    below = moved(pack, layers, peers, lambda layer, place: (layer - 1, place) if layer else None)

    def apply(layer, groups, couple, kept, going_down, turning):
        total = None
        for group in groups[:-1]:
            pairs = group(total)
            total = partial_apply(layer, gt, [b for b, _ in pairs], [s for _, s in pairs], total)
        pairs = groups[-1](total)
        blocks, shifts = [b for b, _ in pairs], [s for _, s in pairs]
        return last_apply(layer, gt, blocks, shifts, total, couple, kept, going_down, turning)

    kept = result = None
    for layer in range(layers):
        turning = layer == layers - 1
        if layer:
            kept = result if layer == 1 else keep(layer - 1, gt, kept, result)
        couple = coupling if turning else fetch(gt, below, result) if layer else below
        result, sent = apply(layer, groups, couple, kept, True, turning)
        groups = arrive(sent, layer ^ (layer - 1 if turning else layer + 1))
    for layer in range(layers - 2, -1, -1):
        kept = keep(layer + 1, gt, kept, result)
        result, *sent = apply(layer, groups, coupling, kept, False, False)
        if layer:
            groups = arrive(sent[0], layer ^ (layer - 1))
    return result


def solution(mesh):
    layers, peers = mesh.shape["depth"], mesh.shape["front"]
    placed = (
        P("depth", None, "front", None),
        P("depth", "front"),
        P("depth", None, None, "front"),
        P(None, None, "front"),
    )

    def body(inverse_factor, coupling, forcing, upper_trace):
        rows = inverse_factor.shape[2]
        fits = inverse_factor.size * 2 <= 40 << 20 and rows % WIDE == 0
        if fits and peers in (2, 4, 8) and layers in (2, 4, 8):
            return resident_body(layers, peers, inverse_factor, coupling, forcing, upper_trace)
        return plain_body(inverse_factor, coupling, forcing, upper_trace)

    return jax.shard_map(
        body, mesh=mesh, in_specs=placed, out_specs=P("depth", None, None, "front"), check_vma=False
    )
```
